256 devices in a mesh: ep: 32 (over y, x, core), cp: 2 (over z_lo), tp: 4 (over z_hi).
Axes of the slice: x: 4, y: 4, z: 8 (z_hi: 4, z_lo: 2; z = z_hi * 2 + z_lo), core: 2. Of those that a mesh axis runs over, the one named last changes fastest.
Arguments:
- tokens: bfloat16 [4096, 7168], P(('ep', 'cp', 'tp')), may hold values from -6 to 6
- cotangent: bfloat16 [4096, 7168], P(('ep', 'cp', 'tp')), may hold values from -6 to 6
- routes: int32 [4096, 8], P(('ep', 'cp', 'tp')), may hold values from 0 to 63, all different within a row; in each aligned block of 128 rows (0 to 127, 128 to 255, ...) at most 20 rows name the same one
- route_weights: float32 [4096, 8], P(('ep', 'cp', 'tp')), may hold values from 0.05 to 0.5
- gate_weight: bfloat16 [64, 7168, 1024], P('ep', ('cp', 'tp')), may hold values from -0.0625 to 0.0625
- up_weight: bfloat16 [64, 7168, 1024], P('ep', ('cp', 'tp')), may hold values from -0.0625 to 0.0625
- down_weight: bfloat16 [64, 1024, 7168], P('ep', None, ('cp', 'tp')), may hold values from -0.1875 to 0.1875
Outputs:
- mixed: bfloat16 [4096, 7168], P(('ep', 'cp', 'tp'))
- input_grad: bfloat16 [4096, 7168], P(('ep', 'cp', 'tp'))
The draws below stay inside these ranges and needn't reach their ends.
Inputs may be any that keep to these rules, and one draw needn't show every extreme that they name: `routes`: each row names 8 different experts. In each aligned block of 128 rows (the tokens of one index of ep) no expert is named by more than 20 rows, a bound that some block reaches.
All inputs are finite; a program needn't handle non-finite values.
Results may differ from the reference program's by a relative error of at most 0.029.
Values may be sent and summed in bfloat16 or wider, within the bound.
No kernel may reach another device: no remote copies, remote signals or barrier semaphores. Data moves between devices by JAX's collectives and lax.ppermute only.
A program may use at most 128 MiB of HBM per device.

```python
import math
import jax
import jax.numpy as jnp
import numpy as np
from jax import lax

D = 7168
TOPK = 8
FF = 1024
EXPERTS = 64
TOKENS = 4096
GROUP_TOK = 128
MOST = 20
N_EP = 32
N_CP = 2
N_TP = 4


def steps_of(stream_key, dims, pieces, least, largest):
    factor_of = 1.0
    for axis_at, shards_of in pieces:
        draws = jax.random.uniform(jax.random.fold_in(jax.random.fold_in(stream_key, 6), axis_at), (shards_of,), jnp.float32, least / len(pieces), largest / len(pieces))
        factor_of = factor_of * jnp.repeat(jnp.exp(draws), dims[axis_at] // shards_of).reshape((-1,) + (1,) * (len(dims) - 1 - axis_at))
    return factor_of


def deal_out(key, own, number, rows, number_of, top, limit, slope):
    sequence = jax.random.permutation(key, number_of)
    heavy_load, usual = shares(number_of, rows * top, limit, slope, True), shares(number_of, rows * top, limit, slope, False)
    places = jnp.arange(number_of)

    def named(lengths, rotation):
        used = int((lengths > 0).sum())
        fixed = max(1, used // 4)
        moved = fixed + (places - fixed + rotation * (used - fixed)) % max(1, number_of - fixed)
        return jnp.zeros((number_of,), jnp.int32).at[sequence[jnp.where(places < fixed, places, moved)]].set(jnp.asarray(lengths, jnp.int32))

    lengths = jnp.where(number % 4 == 0, named(heavy_load, number // 4), named(usual, number - number // 4 - 1))
    mixed = jax.random.permutation(jax.random.fold_in(own, 3), number_of)
    donor, taker = mixed[0:number_of // 2 * 2:2], mixed[1:number_of // 2 * 2:2]
    slack = jnp.minimum(lengths[donor] - 1, limit - lengths[taker]) // 2
    slack = jnp.where((donor == sequence[0]) | (taker == sequence[0]) | (lengths[taker] == 0), 0, jnp.maximum(slack, 0))
    moved = jax.random.randint(jax.random.fold_in(own, 4), (number_of // 2,), 0, 1 << 20) % (slack + 1)
    lengths = lengths.at[donor].add(-moved).at[taker].add(moved)
    members = jnp.searchsorted(jnp.cumsum(lengths), jnp.arange(rows * top), side="right").astype(jnp.int32)
    grid = members.reshape(top, rows).T
    grid = grid[jax.random.permutation(jax.random.fold_in(own, 1), rows)]
    rotation = jax.random.randint(jax.random.fold_in(own, 2), (rows, 1), 0, top)
    return jnp.take_along_axis(grid, (jnp.arange(top)[None, :] + rotation) % top, axis=1)


def shares(number_of, total, reach, skew, full):
    weights = [(1 << 20) // math.isqrt(standing ** skew) + 1 for standing in range(1, number_of + 1)]
    largest = reach if full else min(reach, max(-(-total // number_of), total * weights[0] // sum(weights)))
    least = 1 if total - largest >= number_of - 1 else 0
    given, spare = [largest] + [least] * (number_of - 1), total - largest - least * (number_of - 1)
    while spare > 0:
        candidates = [i for i in range(1, number_of) if given[i] < largest] or [i for i in range(1, number_of) if given[i] < reach]
        mass, left = sum([weights[i] for i in candidates]), spare
        for i in candidates:
            more = min(reach - given[i], max(1, left * weights[i] // mass), spare)
            given[i] = given[i] + more
            spare = spare - more
    return np.array(given)


def bell_draw(key, shape, scale, limit, cuts=(), kind=jnp.bfloat16):
    gain = steps_of(key, shape, cuts, -0.22, 0.18) if cuts else 1.0
    drawn = jax.random.normal(key, shape, jnp.float32) * scale * gain
    return jnp.minimum(jnp.maximum(drawn, -limit), limit).astype(kind)


def setup_inputs(seed: int = 0) -> dict:
    key_of = jax.random.split(jax.random.key(seed), 8)
    tokens = bell_draw(key_of[0], (TOKENS, D), 1.0, 6.0, ((0, 256),))
    cotangent = bell_draw(key_of[1], (TOKENS, D), 1.0, 6.0, ((0, 256),))
    routes_keys = jax.random.split(jax.random.fold_in(key_of[2], 1), TOKENS // GROUP_TOK)
    routes_turns = jax.random.permutation(jax.random.fold_in(key_of[2], 3), TOKENS // GROUP_TOK)
    routes = jax.vmap(lambda own, number: deal_out(jax.random.fold_in(key_of[2], 2), own, number, GROUP_TOK, EXPERTS, TOPK, MOST, 2))(routes_keys, routes_turns).reshape((TOKENS, TOPK))
    route_weights = jnp.clip(jnp.exp(math.log(0.5) - 2.3025851 * jax.random.uniform(key_of[3], (TOKENS, TOPK), jnp.float32) ** steps_of(key_of[3], (TOKENS, TOPK), ((0, 256),), -0.2, 0.2)), 0.05, 0.5)
    gate_weight = bell_draw(key_of[4], (EXPERTS, D, FF), D ** -0.5, 0.0625, ((0, 32), (1, 8)))
    up_weight = bell_draw(key_of[5], (EXPERTS, D, FF), D ** -0.5, 0.0625, ((0, 32), (1, 8)))
    down_weight = bell_draw(key_of[6], (EXPERTS, FF, D), FF ** -0.5, 0.1875, ((0, 32), (2, 8)))
    return {"tokens": tokens, "cotangent": cotangent, "routes": routes, "route_weights": route_weights, "gate_weight": gate_weight, "up_weight": up_weight, "down_weight": down_weight}


def rounded(values):
    return lax.optimization_barrier(values.astype(jnp.bfloat16)).astype(jnp.float32)


def expert_rows(tok_rows, grad_rows, gate_mat, up_mat, down_mat, blocks):
    count = tok_rows.shape[0]
    width = tok_rows.shape[1] // blocks
    units = gate_mat.shape[1]
    tok_split = tok_rows.astype(jnp.float32).reshape(count, blocks, width)
    grad_split = grad_rows.astype(jnp.float32).reshape(count, blocks, width)
    gate_split = gate_mat.astype(jnp.float32).reshape(blocks, width, units)
    up_split = up_mat.astype(jnp.float32).reshape(blocks, width, units)
    down_split = down_mat.astype(jnp.float32).reshape(units, blocks, width)
    gate = jnp.sum(rounded(jnp.einsum("rbd,bdf->rbf", tok_split, gate_split)), axis=1)
    upper = jnp.sum(rounded(jnp.einsum("rbd,bdf->rbf", tok_split, up_split)), axis=1)
    back = jnp.sum(rounded(jnp.einsum("rbd,fbd->rbf", grad_split, down_split)), axis=1)
    sigmoid_gate = jax.nn.sigmoid(gate)
    activated = gate * sigmoid_gate
    hidden_act = (activated * upper).astype(jnp.bfloat16)
    d_up = (back * activated).astype(jnp.bfloat16)
    d_gate = (back * upper * sigmoid_gate * (1.0 + gate * (1.0 - sigmoid_gate))).astype(jnp.bfloat16)
    out_rows = jnp.dot(hidden_act, down_mat, preferred_element_type=jnp.float32).astype(jnp.bfloat16)
    grad_out = (jnp.dot(d_gate, gate_mat.T, preferred_element_type=jnp.float32)
                + jnp.dot(d_up, up_mat.T, preferred_element_type=jnp.float32)).astype(jnp.bfloat16)
    return out_rows, grad_out


def reference(tokens, cotangent, routes, route_weights, gate_weight, up_weight, down_weight):
    flat_routes = routes.reshape(-1).astype(jnp.int32)
    flat_weights = route_weights.reshape(-1).astype(jnp.float32)
    capacity = N_EP * MOST
    blocks = N_CP * N_TP
    order = jnp.argsort(flat_routes, stable=True).astype(jnp.int32)
    expert_ids = jnp.arange(EXPERTS, dtype=jnp.int32)
    counts = jnp.sum((flat_routes[:, None] == expert_ids[None, :]).astype(jnp.int32), axis=0).astype(jnp.int32)
    starts = (jnp.cumsum(counts) - counts).astype(jnp.int32)
    padded_order = jnp.concatenate([order, jnp.zeros((capacity,), jnp.int32)])

    def one_expert(carry, expert):
        mixed, input_grad = carry
        picked = lax.dynamic_slice(padded_order, (starts[expert].astype(jnp.int32),), (capacity,))
        valid = jnp.arange(capacity, dtype=jnp.int32) < counts[expert]
        token = (picked // TOPK).astype(jnp.int32)
        out_rows, grad_out = expert_rows(tokens[token], cotangent[token], gate_weight[expert],
                                         up_weight[expert], down_weight[expert], blocks)
        scale = jnp.where(valid, flat_weights[picked], jnp.zeros((capacity,), jnp.float32))[:, None]
        mixed = mixed.at[token].add(scale * out_rows.astype(jnp.float32))
        input_grad = input_grad.at[token].add(scale * grad_out.astype(jnp.float32))
        return (mixed, input_grad), None

    start_state = (jnp.zeros((TOKENS, D), jnp.float32), jnp.zeros((TOKENS, D), jnp.float32))
    (mixed, input_grad), _ = lax.scan(one_expert, start_state, expert_ids)
    return mixed.astype(jnp.bfloat16), input_grad.astype(jnp.bfloat16)
```

```python
import jax
import jax.numpy as jnp
from jax import lax
from jax.sharding import PartitionSpec as P

BF = jnp.bfloat16
F32 = jnp.float32
Z = ("cp", "tp")
ALL = ("ep", "cp", "tp")


def ring_pairs(step):
    cp, tp = lax.axis_size("cp"), lax.axis_size("tp")
    count = cp * tp

    def place(z):
        z = z % count
        return (z % cp) * tp + z // cp

    return [(place(z), place(z + step)) for z in range(count)]


def ring_place():
    return lax.axis_index("tp") * lax.axis_size("cp") + lax.axis_index("cp")


def chunk_of(part, index):
    count = part.shape[0]
    return lax.dynamic_index_in_dim(part, lax.rem(index + 2 * count, count), 0, keepdims=False)


def ring_sum(parts, steps):
    count = parts[0].shape[0]
    place, pairs = ring_place(), [ring_pairs(step) for step in steps]
    totals = [chunk_of(part, place - step) for part, step in zip(parts, steps)]
    for hop in range(count - 1):
        got = [lax.ppermute(total, Z, pair) for total, pair in zip(totals, pairs)]
        own = [chunk_of(part, place - step * (2 + hop)) for part, step in zip(parts, steps)]
        totals = [(g.astype(F32) + o.astype(F32)).astype(BF) for g, o in zip(got, own)]
    return totals


def ring_spread(chunks, steps, count):
    place, pairs = ring_place(), [ring_pairs(step) for step in steps]
    wholes = [jnp.zeros((count,) + chunk.shape, chunk.dtype) for chunk in chunks]
    for hop in range(count):
        if hop:
            chunks = [lax.ppermute(chunk, Z, pair) for chunk, pair in zip(chunks, pairs)]
        at = [lax.rem(place - step * hop + 2 * count, count) for step in steps]
        wholes = [lax.dynamic_update_index_in_dim(w, c, i, 0) for w, c, i in zip(wholes, chunks, at)]
    return wholes


def after(x, *others):
    return lax.optimization_barrier((x,) + others)[0]


def hidden_units(gate, upper):
    gate, upper = gate.astype(F32), upper.astype(F32)
    return (gate * jax.nn.sigmoid(gate) * upper).astype(BF)


def grad_units(gate, upper, back):
    gate, upper, back = gate.astype(F32), upper.astype(F32), back.astype(F32)
    sigmoid_gate = jax.nn.sigmoid(gate)
    d_up = (back * gate * sigmoid_gate).astype(BF)
    d_gate = (back * upper * sigmoid_gate * (1.0 + gate * (1.0 - sigmoid_gate))).astype(BF)
    return d_gate, d_up


def dot(a, b, dims):
    return lax.dot_general(a, b, (dims, ((), ())), preferred_element_type=F32)


def shards(tokens, cotangent, routes, route_weights, gate_weight, up_weight, down_weight):
    ep = lax.axis_size("ep")
    ring = lax.axis_size("cp") * lax.axis_size("tp")
    local, width, units = gate_weight.shape
    own_tok, top = routes.shape
    group = own_tok * ring
    experts = local * ep
    slots = min(group, 5 * group * top // (4 * experts))
    rows = ep * slots

    high = lax.reduce_precision(route_weights, 8, 7)
    low = route_weights - high
    meta = jnp.concatenate([routes.astype(BF), high.astype(BF), low.astype(BF)], axis=1)
    meta = jnp.pad(meta, ((0, 0), (0, 128 - 3 * top)))
    tok_out = jnp.concatenate(
        [
            tokens.reshape(own_tok, ring, width).transpose(1, 0, 2),
            jnp.broadcast_to(meta[None], (ring, own_tok, 128)),
        ],
        axis=2,
    )
    tok_in = lax.all_to_all(tok_out, Z, split_axis=0, concat_axis=0, tiled=True).reshape(group, width + 128)
    tok_cols = tok_in[:, :width]
    meta = tok_in[:, width:]
    group_routes = meta[:, :top].astype(jnp.int32)
    group_weights = meta[:, top : 2 * top].astype(F32) + meta[:, 2 * top : 3 * top].astype(F32)

    named = group_routes[:, :, None] == jnp.arange(experts, dtype=jnp.int32)
    mask = jnp.any(named, axis=1)
    weight = jnp.sum(jnp.where(named, group_weights[:, :, None], 0.0), axis=1)
    before = jnp.arange(group)[None, :] < jnp.arange(group)[:, None]
    position = dot(mask.astype(BF), before.astype(BF), ((0,), (1,))).astype(jnp.int32)
    position = jnp.where(mask.T, position, -1).reshape(ep, local, 1, group)
    slot = jnp.arange(slots, dtype=jnp.int32)
    hit = position == slot[:, None]
    spread = hit.astype(BF)
    scaled = jnp.where(hit, weight.T.reshape(ep, local, 1, group), 0.0).reshape(local * rows, group)
    top_term = lax.reduce_precision(scaled, 8, 7)
    gather = (top_term.astype(BF), (scaled - top_term).astype(BF))

    def over_ep(out):
        return lax.all_to_all(out, "ep", split_axis=0, concat_axis=0, tiled=True)

    tok_rows, parts = [], []
    for e in range(local):
        out = dot(spread[:, e].reshape(rows, group), tok_cols, ((1,), (0,))).astype(BF)
        if e:
            out = after(out, *parts[0])
        tok_rows.append(over_ep(out.reshape(ep, slots, width)).reshape(rows, width))
        parts.append([dot(tok_rows[e], w[e], ((1,), (0,))).astype(BF) for w in (gate_weight, up_weight)])
    cotangent = after(cotangent, tok_rows[-1])
    grad_out = cotangent.reshape(own_tok, ring, width).transpose(1, 0, 2)
    grad_cols = lax.all_to_all(grad_out, Z, split_axis=0, concat_axis=0, tiled=True).reshape(group, width)
    out = dot(spread.reshape(local * rows, group), grad_cols, ((1,), (0,)))
    grad_rows = over_ep(out.astype(BF).reshape(ep, local * slots, width)).reshape(ep, local, slots, width)

    first = [lax.psum(part, Z) for part in parts[0]]
    ways = (1, -1)
    second = ring_sum([part.reshape(ring, rows // ring, units) for part in parts[1]], ways)
    back_parts = [
        dot(grad_rows[:, e].reshape(rows, width), down_weight[e], ((1,), (1,))).astype(BF) for e in range(local)
    ]
    second = [after(chunk, *first, *back_parts) for chunk in second]
    backs = [lax.psum(after(part, *first), Z) for part in back_parts]
    second = [whole.reshape(rows, units) for whole in ring_spread(second, ways, ring)]
    gates, uppers = zip(first, second)
    hiddens = [hidden_units(g, u) for g, u in zip(gates, uppers)]

    def give_back(outs):
        out = jnp.stack([o.astype(BF).reshape(ep, slots, width) for o in outs], axis=1)
        return over_ep(out.reshape(ep, local * slots, width)).reshape(local * rows, width)

    def combine(out):
        return (dot(gather[0], out, ((0,), (0,))) + dot(gather[1], out, ((0,), (0,)))).astype(BF)

    out_back = give_back([dot(hiddens[e], down_weight[e], ((1,), (0,))) for e in range(local)])
    outs = []
    for e in range(local):
        d_gate, d_up = grad_units(gates[e], uppers[e], after(backs[e], out_back))
        outs.append(dot(d_gate, gate_weight[e], ((1,), (1,))) + dot(d_up, up_weight[e], ((1,), (1,))))
    grad_back = give_back(outs)
    cols = jnp.stack([combine(out_back), combine(grad_back)], axis=1).reshape(ring, own_tok, 2, width)
    mine = lax.all_to_all(cols, Z, split_axis=0, concat_axis=0, tiled=True)
    return (
        mine[:, :, 0].transpose(1, 0, 2).reshape(own_tok, ring * width),
        mine[:, :, 1].transpose(1, 0, 2).reshape(own_tok, ring * width),
    )


def solution(mesh):
    in_specs = (
        P(ALL, None),
        P(ALL, None),
        P(ALL, None),
        P(ALL, None),
        P("ep", Z, None),
        P("ep", Z, None),
        P("ep", None, Z),
    )
    out_specs = (P(ALL, None), P(ALL, None))
    return jax.shard_map(shards, mesh=mesh, in_specs=in_specs, out_specs=out_specs, check_vma=False)
```

```python
import jax
import jax.numpy as jnp
from jax import lax
from jax.experimental import pallas as pl
from jax.experimental.pallas import tpu as pltpu
from jax.sharding import PartitionSpec as P

BF = jnp.bfloat16
F32 = jnp.float32
Z = ("cp", "tp")
ALL = ("ep", "cp", "tp")


def ring_pairs(step):
    cp, tp = lax.axis_size("cp"), lax.axis_size("tp")
    count = cp * tp

    def place(z):
        z = z % count
        return (z % cp) * tp + z // cp

    return [(place(z), place(z + step)) for z in range(count)]


def ring_place():
    return lax.axis_index("tp") * lax.axis_size("cp") + lax.axis_index("cp")


def chunk_of(part, index):
    count = part.shape[0]
    return lax.dynamic_index_in_dim(part, lax.rem(index + 2 * count, count), 0, keepdims=False)


def ring_sum(parts, steps, ties):
    count = parts[0].shape[0]
    place, pairs = ring_place(), [ring_pairs(step) for step in steps]
    totals = [chunk_of(part, place - step) for part, step in zip(parts, steps)]
    for hop in range(count - 1):
        totals = [after(total, *ties.get(hop, ())) for total in totals]
        got = [lax.ppermute(total, Z, pair) for total, pair in zip(totals, pairs)]
        own = [chunk_of(part, place - step * (2 + hop)) for part, step in zip(parts, steps)]
        totals = [(g.astype(F32) + o.astype(F32)).astype(BF) for g, o in zip(got, own)]
    return totals


def ring_spread(chunks, steps, count):
    place, pairs = ring_place(), [ring_pairs(step) for step in steps]
    wholes = [jnp.zeros((count,) + chunk.shape, chunk.dtype) for chunk in chunks]
    for hop in range(count):
        if hop:
            chunks = [lax.ppermute(chunk, Z, pair) for chunk, pair in zip(chunks, pairs)]
        at = [lax.rem(place - step * hop + 2 * count, count) for step in steps]
        wholes = [lax.dynamic_update_index_in_dim(w, c, i, 0) for w, c, i in zip(wholes, chunks, at)]
    return wholes


def after(x, *others):
    if not others:
        return x
    return lax.optimization_barrier((x,) + others)[0]


def dot(a, b, dims):
    return lax.dot_general(a, b, (dims, ((), ())), preferred_element_type=F32)


def output_kernel(*refs):
    (gate0, gate1, up0, up1, down, order, out) = refs
    rows = []
    for e, (gate, upper) in enumerate(((gate0, up0), (gate1, up1))):
        gate, upper = gate[...].astype(F32), upper[...].astype(F32)
        hidden = (gate * jax.nn.sigmoid(gate) * upper).astype(BF)
        rows.append(dot(hidden, down[e], ((1,), (0,))).astype(BF))
    out[...] = dot(order[...], jnp.concatenate(rows, axis=0), ((1,), (0,))).astype(BF)


def grad_kernel(*refs):
    (gate0, gate1, up0, up1, back0, back1, gate_w, up_w, order, out) = refs
    rows = []
    for e, (gate, upper, back) in enumerate(((gate0, up0, back0), (gate1, up1, back1))):
        gate, upper, back = (x[...].astype(F32) for x in (gate, upper, back))
        sig = jax.nn.sigmoid(gate)
        d_up = (back * gate * sig).astype(BF)
        d_gate = (back * upper * sig * (1.0 + gate * (1.0 - sig))).astype(BF)
        grad = dot(d_gate, gate_w[e], ((1,), (1,))) + dot(d_up, up_w[e], ((1,), (1,)))
        rows.append(grad.astype(BF))
    out[...] = dot(order[...], jnp.concatenate(rows, axis=0), ((1,), (0,))).astype(BF)


def expert_rows(kernel, sums, weights, slots):
    rows, units = sums[0][0].shape
    local = weights[0].shape[0]
    width = weights[0].size // (local * units)
    block = 8 * slots
    inputs = [x for pair in sums for x in pair]
    row = jnp.arange(local * block)
    sender, inner = row // (local * slots), row % (local * slots)
    source = (inner // slots) * block + sender * slots + inner % slots
    order = (source[:, None] == row[None, :]).astype(BF)
    flops = 2 * local * rows * units * width * len(weights)
    return pl.pallas_call(
        kernel,
        grid=(rows // block,),
        in_specs=[pl.BlockSpec((block, units), lambda i: (i, 0))] * len(inputs)
        + [pl.BlockSpec(w.shape, lambda i: (0, 0, 0)) for w in weights]
        + [pl.BlockSpec(order.shape, lambda i: (0, 0))],
        out_specs=pl.BlockSpec((local * block, width), lambda i: (i, 0)),
        out_shape=jax.ShapeDtypeStruct((local * rows, width), BF),
        compiler_params=pltpu.CompilerParams(vmem_limit_bytes=50 * 1024 * 1024),
        cost_estimate=pl.CostEstimate(flops=flops, bytes_accessed=12 * 1024 * 1024, transcendentals=local * rows * units),
    )(*inputs, *weights, order)


def shards(tokens, cotangent, routes, route_weights, gate_weight, up_weight, down_weight):
    ep = lax.axis_size("ep")
    ring = lax.axis_size("cp") * lax.axis_size("tp")
    local, width, units = gate_weight.shape
    own_tok, top = routes.shape
    group = own_tok * ring
    experts = local * ep
    slots = min(group, 5 * group * top // (4 * experts))
    rows = ep * slots

    high = lax.reduce_precision(route_weights, 8, 7)
    low = route_weights - high
    meta = jnp.concatenate([routes.astype(BF), high.astype(BF), low.astype(BF)], axis=1)
    meta = jnp.pad(meta, ((0, 0), (0, 128 - 3 * top)))
    tok_out = jnp.concatenate(
        [
            tokens.reshape(own_tok, ring, width).transpose(1, 0, 2),
            jnp.broadcast_to(meta[None], (ring, own_tok, 128)),
        ],
        axis=2,
    )
    tok_in = lax.all_to_all(tok_out, Z, split_axis=0, concat_axis=0, tiled=True).reshape(group, width + 128)
    tok_cols = tok_in[:, :width]
    meta = tok_in[:, width:]
    group_routes = meta[:, :top].astype(jnp.int32)
    group_weights = meta[:, top : 2 * top].astype(F32) + meta[:, 2 * top : 3 * top].astype(F32)

    named = group_routes[:, :, None] == jnp.arange(experts, dtype=jnp.int32)
    mask = jnp.any(named, axis=1)
    weight = jnp.sum(jnp.where(named, group_weights[:, :, None], 0.0), axis=1)
    before = jnp.arange(group)[None, :] < jnp.arange(group)[:, None]
    position = dot(mask.astype(BF), before.astype(BF), ((0,), (1,))).astype(jnp.int32)
    position = jnp.where(mask.T, position, -1).reshape(ep, local, 1, group)
    slot = jnp.arange(slots, dtype=jnp.int32)
    hit = position == slot[:, None]
    spread = hit.astype(BF)
    scaled = jnp.where(hit, weight.T.reshape(ep, local, 1, group), 0.0).reshape(local * rows, group)
    top_term = lax.reduce_precision(scaled, 8, 7)
    gather = jnp.concatenate([top_term.astype(BF), (scaled - top_term).astype(BF)], axis=1)

    def over_ep(out):
        return lax.all_to_all(out, "ep", split_axis=0, concat_axis=0, tiled=True)

    tok_rows, parts = [], []
    for e in range(local):
        out = dot(spread[:, e].reshape(rows, group), tok_cols, ((1,), (0,))).astype(BF)
        if e:
            out = after(out, *parts[0])
        tok_rows.append(over_ep(out.reshape(ep, slots, width)).reshape(rows, width))
        parts.append([dot(tok_rows[e], w[e], ((1,), (0,))).astype(BF) for w in (gate_weight, up_weight)])
    cotangent = after(cotangent, tok_rows[-1])
    grad_out = cotangent.reshape(own_tok, ring, width).transpose(1, 0, 2)
    grad_cols = lax.all_to_all(grad_out, Z, split_axis=0, concat_axis=0, tiled=True).reshape(group, width)
    out = dot(spread.reshape(local * rows, group), grad_cols, ((1,), (0,)))
    grad_send = out.astype(BF).reshape(ep, local * slots, width)
    grad_rows = over_ep(grad_send).reshape(ep, local, slots, width)

    first = [lax.psum(part, Z) for part in parts[0]]
    ways = (1, -1)
    back_parts = [
        dot(grad_rows[:, e].reshape(rows, width), down_weight[e], ((1,), (1,))).astype(BF) for e in range(local)
    ]
    second = ring_sum(
        [part.reshape(ring, rows // ring, units) for part in parts[1]], ways, {1: (grad_send,), 5: back_parts}
    )
    second = [after(chunk, *first) for chunk in second]
    backs = [lax.psum(after(part, *first), Z) for part in back_parts]
    second = [whole.reshape(rows, units) for whole in ring_spread(second, ways, ring)]
    gates, uppers = zip(first, second)

    def give_back(out):
        return over_ep(out.reshape(ep, local * slots, width)).reshape(local * rows, width)

    def combine(out):
        both = dot(gather, out, ((0,), (0,)))
        return (both[:group] + both[group:]).astype(BF)

    out_back = give_back(
        expert_rows(output_kernel, [gates, uppers], [down_weight], slots)
    )
    grads = expert_rows(grad_kernel, [gates, uppers, backs], [gate_weight, up_weight], slots)
    grad_back = give_back(after(grads, out_back))
    cols = jnp.stack([combine(out_back), combine(grad_back)], axis=1).reshape(ring, own_tok, 2, width)
    mine = lax.all_to_all(cols, Z, split_axis=0, concat_axis=0, tiled=True)
    return (
        mine[:, :, 0].transpose(1, 0, 2).reshape(own_tok, ring * width),
        mine[:, :, 1].transpose(1, 0, 2).reshape(own_tok, ring * width),
    )


def solution(mesh):
    in_specs = (
        P(ALL, None),
        P(ALL, None),
        P(ALL, None),
        P(ALL, None),
        P("ep", Z, None),
        P("ep", Z, None),
        P("ep", None, Z),
    )
    out_specs = (P(ALL, None), P(ALL, None))
    return jax.shard_map(shards, mesh=mesh, in_specs=in_specs, out_specs=out_specs, check_vma=False)
```

```python
import jax
import jax.numpy as jnp
from jax import lax
from jax.experimental import pallas as pl
from jax.experimental.pallas import tpu as pltpu
from jax.sharding import PartitionSpec as P

BF = jnp.bfloat16
F32 = jnp.float32
Z = ("cp", "tp")
ALL = ("ep", "cp", "tp")


def ring_pairs(step):
    cp, tp = lax.axis_size("cp"), lax.axis_size("tp")
    count = cp * tp

    def place(z):
        z = z % count
        return (z % cp) * tp + z // cp

    return [(place(z), place(z + step)) for z in range(count)]


def ring_place():
    return lax.axis_index("tp") * lax.axis_size("cp") + lax.axis_index("cp")


def chunk_of(part, index):
    count = part.shape[0]
    return lax.dynamic_index_in_dim(part, lax.rem(index + 2 * count, count), 0, keepdims=False)


def ring_sum(parts, steps, ties):
    count = parts[0].shape[0]
    place, pairs = ring_place(), [ring_pairs(step) for step in steps]
    totals = [chunk_of(part, place - step) for part, step in zip(parts, steps)]
    for hop in range(count - 1):
        totals = [after(total, *ties.get(hop, ())) for total in totals]
        got = [lax.ppermute(total, Z, pair) for total, pair in zip(totals, pairs)]
        own = [chunk_of(part, place - step * (2 + hop)) for part, step in zip(parts, steps)]
        totals = [(g.astype(F32) + o.astype(F32)).astype(BF) for g, o in zip(got, own)]
    return totals


def ring_spread(chunks, steps, count):
    place, pairs = ring_place(), [ring_pairs(step) for step in steps]
    wholes = [jnp.zeros((count,) + chunk.shape, chunk.dtype) for chunk in chunks]
    for hop in range(count):
        if hop:
            chunks = [lax.ppermute(chunk, Z, pair) for chunk, pair in zip(chunks, pairs)]
        at = [lax.rem(place - step * hop + 2 * count, count) for step in steps]
        wholes = [lax.dynamic_update_index_in_dim(w, c, i, 0) for w, c, i in zip(wholes, chunks, at)]
    return wholes


def after(x, *others):
    if not others:
        return x
    return lax.optimization_barrier((x,) + others)[0]


def dot(a, b, dims):
    return lax.dot_general(a, b, (dims, ((), ())), preferred_element_type=F32)


def interleave(rows, order, out):
    step = order.shape[0]
    piece = step // len(rows)
    for i in range(out.shape[0] // step):
        both = jnp.concatenate([r[i * piece : (i + 1) * piece] for r in rows], axis=0)
        out[i * step : (i + 1) * step, :] = dot(order[...], both, ((1,), (0,))).astype(BF)


def output_kernel(*refs):
    (gate0, gate1, up0, up1, down, order, out) = refs
    rows = []
    for e, (gate, upper) in enumerate(((gate0, up0), (gate1, up1))):
        gate, upper = gate[...].astype(F32), upper[...].astype(F32)
        hidden = (gate * jax.nn.sigmoid(gate) * upper).astype(BF)
        rows.append(dot(hidden, down[e], ((1,), (0,))).astype(BF))
    interleave(rows, order, out)


def grad_kernel(*refs):
    (gate0, gate1, up0, up1, back0, back1, gate_w, up_w, order, out) = refs
    rows = []
    for e, (gate, upper, back) in enumerate(((gate0, up0, back0), (gate1, up1, back1))):
        gate, upper, back = (x[...].astype(F32) for x in (gate, upper, back))
        sig = jax.nn.sigmoid(gate)
        d_up = (back * gate * sig).astype(BF)
        d_gate = (back * upper * sig * (1.0 + gate * (1.0 - sig))).astype(BF)
        grad = dot(d_gate, gate_w[e], ((1,), (1,))) + dot(d_up, up_w[e], ((1,), (1,)))
        rows.append(grad.astype(BF))
    interleave(rows, order, out)


def expert_rows(kernel, sums, weights, slots):
    rows, units = sums[0][0].shape
    local = weights[0].shape[0]
    width = weights[0].size // (local * units)
    block = 8 * slots
    step = 2 * block
    inputs = [x for pair in sums for x in pair]
    row = jnp.arange(local * block)
    sender, inner = row // (local * slots), row % (local * slots)
    source = (inner // slots) * block + sender * slots + inner % slots
    order = (source[:, None] == row[None, :]).astype(BF)
    flops = 2 * local * rows * units * width * len(weights)
    return pl.pallas_call(
        kernel,
        grid=(rows // step,),
        in_specs=[pl.BlockSpec((step, units), lambda i: (i, 0))] * len(inputs)
        + [pl.BlockSpec(w.shape, lambda i: (0, 0, 0)) for w in weights]
        + [pl.BlockSpec(order.shape, lambda i: (0, 0))],
        out_specs=pl.BlockSpec((local * step, width), lambda i: (i, 0)),
        out_shape=jax.ShapeDtypeStruct((local * rows, width), BF),
        compiler_params=pltpu.CompilerParams(vmem_limit_bytes=50 * 1024 * 1024),
        cost_estimate=pl.CostEstimate(flops=flops, bytes_accessed=12 * 1024 * 1024, transcendentals=local * rows * units),
    )(*inputs, *weights, order)


def shards(tokens, cotangent, routes, route_weights, gate_weight, up_weight, down_weight):
    ep = lax.axis_size("ep")
    ring = lax.axis_size("cp") * lax.axis_size("tp")
    local, width, units = gate_weight.shape
    own_tok, top = routes.shape
    group = own_tok * ring
    experts = local * ep
    slots = min(group, 5 * group * top // (4 * experts))
    rows = ep * slots

    high = lax.reduce_precision(route_weights, 8, 7)
    low = route_weights - high
    meta = jnp.concatenate([routes.astype(BF), high.astype(BF), low.astype(BF)], axis=1)
    meta = jnp.pad(meta, ((0, 0), (0, 128 - 3 * top)))
    tok_out = jnp.concatenate(
        [
            tokens.reshape(own_tok, ring, width).transpose(1, 0, 2),
            cotangent.reshape(own_tok, ring, width).transpose(1, 0, 2),
            jnp.broadcast_to(meta[None], (ring, own_tok, 128)),
        ],
        axis=2,
    )
    tok_in = lax.all_to_all(tok_out, Z, split_axis=0, concat_axis=0, tiled=True).reshape(group, 2 * width + 128)
    tok_cols = tok_in[:, :width]
    grad_cols = tok_in[:, width : 2 * width]
    meta = tok_in[:, 2 * width :]
    group_routes = meta[:, :top].astype(jnp.int32)
    group_weights = meta[:, top : 2 * top].astype(F32) + meta[:, 2 * top : 3 * top].astype(F32)

    named = group_routes[:, :, None] == jnp.arange(experts, dtype=jnp.int32)
    mask = jnp.any(named, axis=1)
    weight = jnp.sum(jnp.where(named, group_weights[:, :, None], 0.0), axis=1)
    before = jnp.arange(group)[None, :] < jnp.arange(group)[:, None]
    position = dot(mask.astype(BF), before.astype(BF), ((0,), (1,))).astype(jnp.int32)
    position = jnp.where(mask.T, position, -1).reshape(ep, local, 1, group)
    slot = jnp.arange(slots, dtype=jnp.int32)
    hit = position == slot[:, None]
    spread = hit.astype(BF)
    scaled = jnp.where(hit, weight.T.reshape(ep, local, 1, group), 0.0).reshape(local * rows, group)
    top_term = lax.reduce_precision(scaled, 8, 7)
    gather = jnp.concatenate([top_term.astype(BF), (scaled - top_term).astype(BF)], axis=1)

    def over_ep(out):
        return lax.all_to_all(out, "ep", split_axis=0, concat_axis=0, tiled=True)

    tok_rows, parts = [], []
    for e in range(local):
        out = dot(spread[:, e].reshape(rows, group), tok_cols, ((1,), (0,))).astype(BF)
        if e:
            out = after(out, *parts[0])
        tok_rows.append(over_ep(out.reshape(ep, slots, width)).reshape(rows, width))
        parts.append([dot(tok_rows[e], w[e], ((1,), (0,))).astype(BF) for w in (gate_weight, up_weight)])
    grad_cols = after(grad_cols, tok_rows[-1])
    out = dot(spread.reshape(local * rows, group), grad_cols, ((1,), (0,)))
    grad_send = out.astype(BF).reshape(ep, local * slots, width)
    grad_rows = over_ep(grad_send).reshape(ep, local, slots, width)

    first = [lax.psum(part, Z) for part in parts[0]]
    ways = (1, -1)
    back_parts = [
        dot(grad_rows[:, e].reshape(rows, width), down_weight[e], ((1,), (1,))).astype(BF) for e in range(local)
    ]
    second = ring_sum(
        [part.reshape(ring, rows // ring, units) for part in parts[1]], ways, {5: back_parts}
    )
    second = [after(chunk, *first) for chunk in second]
    backs = [lax.psum(part, Z[::-1]) for part in back_parts]
    second = [whole.reshape(rows, units) for whole in ring_spread(second, ways, ring)]
    gates, uppers = zip(first, second)

    def give_back(out):
        return over_ep(out.reshape(ep, local * slots, width)).reshape(local * rows, width)

    def combine(out):
        both = dot(gather, out, ((0,), (0,)))
        return (both[:group] + both[group:]).astype(BF)

    out_back = give_back(
        expert_rows(output_kernel, [gates, uppers], [down_weight], slots)
    )
    grads = expert_rows(grad_kernel, [gates, uppers, backs], [gate_weight, up_weight], slots)
    grad_back = give_back(after(grads, out_back))
    cols = jnp.stack([combine(out_back), combine(grad_back)], axis=1).reshape(ring, own_tok, 2, width)
    mine = lax.all_to_all(cols, Z, split_axis=0, concat_axis=0, tiled=True)
    return (
        mine[:, :, 0].transpose(1, 0, 2).reshape(own_tok, ring * width),
        mine[:, :, 1].transpose(1, 0, 2).reshape(own_tok, ring * width),
    )


def solution(mesh):
    in_specs = (
        P(ALL, None),
        P(ALL, None),
        P(ALL, None),
        P(ALL, None),
        P("ep", Z, None),
        P("ep", Z, None),
        P("ep", None, Z),
    )
    out_specs = (P(ALL, None), P(ALL, None))
    return jax.shard_map(shards, mesh=mesh, in_specs=in_specs, out_specs=out_specs, check_vma=False)
```

```python
import jax
import jax.numpy as jnp
from jax import lax
from jax.experimental import pallas as pl
from jax.experimental.pallas import tpu as pltpu
from jax.sharding import PartitionSpec as P

BF = jnp.bfloat16
F32 = jnp.float32
Z = ("cp", "tp")
ALL = ("ep", "cp", "tp")


def ring_pairs(step):
    cp, tp = lax.axis_size("cp"), lax.axis_size("tp")
    count = cp * tp

    def place(z):
        z = z % count
        return (z % cp) * tp + z // cp

    return [(place(z), place(z + step)) for z in range(count)]


def ring_place():
    return lax.axis_index("tp") * lax.axis_size("cp") + lax.axis_index("cp")


def chunk_of(part, index):
    count = part.shape[0]
    return lax.dynamic_index_in_dim(part, lax.rem(index + 2 * count, count), 0, keepdims=False)


def ring_sum(parts, steps, ties):
    count = parts[0].shape[0]
    place, pairs = ring_place(), [ring_pairs(step) for step in steps]
    totals = [chunk_of(part, place - step) for part, step in zip(parts, steps)]
    for hop in range(count - 1):
        totals = [after(total, *ties.get(hop, ())) for total in totals]
        got = [lax.ppermute(total, Z, pair) for total, pair in zip(totals, pairs)]
        own = [chunk_of(part, place - step * (2 + hop)) for part, step in zip(parts, steps)]
        totals = [(g.astype(F32) + o.astype(F32)).astype(BF) for g, o in zip(got, own)]
    return totals


def ring_spread(chunks, steps, count):
    place, pairs = ring_place(), [ring_pairs(step) for step in steps]
    wholes = [jnp.zeros((count,) + chunk.shape, chunk.dtype) for chunk in chunks]
    for hop in range(count):
        if hop:
            chunks = [lax.ppermute(chunk, Z, pair) for chunk, pair in zip(chunks, pairs)]
        at = [lax.rem(place - step * hop + 2 * count, count) for step in steps]
        wholes = [lax.dynamic_update_index_in_dim(w, c, i, 0) for w, c, i in zip(wholes, chunks, at)]
    return wholes


def after(x, *others):
    if not others:
        return x
    return lax.optimization_barrier((x,) + others)[0]


def dot(a, b, dims):
    return lax.dot_general(a, b, (dims, ((), ())), preferred_element_type=F32)


def interleave(rows, order, out):
    step = order.shape[0]
    piece = step // len(rows)
    for i in range(out.shape[0] // step):
        both = jnp.concatenate([r[i * piece : (i + 1) * piece] for r in rows], axis=0)
        out[i * step : (i + 1) * step, :] = dot(order[...], both, ((1,), (0,))).astype(BF)


def output_kernel(*refs):
    (gate0, gate1, up0, up1, down, order, out) = refs
    rows = []
    for e, (gate, upper) in enumerate(((gate0, up0), (gate1, up1))):
        gate, upper = gate[...].astype(F32), upper[...].astype(F32)
        hidden = (gate * jax.nn.sigmoid(gate) * upper).astype(BF)
        rows.append(dot(hidden, down[e], ((1,), (0,))).astype(BF))
    interleave(rows, order, out)


def grad_kernel(*refs):
    (gate0, gate1, up0, up1, back0, back1, gate_w, up_w, order, out) = refs
    rows = []
    for e, (gate, upper, back) in enumerate(((gate0, up0, back0), (gate1, up1, back1))):
        gate, upper, back = (x[...].astype(F32) for x in (gate, upper, back))
        sig = jax.nn.sigmoid(gate)
        d_up = (back * gate * sig).astype(BF)
        d_gate = (back * upper * sig * (1.0 + gate * (1.0 - sig))).astype(BF)
        grad = dot(d_gate, gate_w[e], ((1,), (1,))) + dot(d_up, up_w[e], ((1,), (1,)))
        rows.append(grad.astype(BF))
    interleave(rows, order, out)


def expert_rows(kernel, sums, weights, slots):
    rows, units = sums[0][0].shape
    local = weights[0].shape[0]
    width = weights[0].size // (local * units)
    block = 8 * slots
    step = 2 * block
    inputs = [x for pair in sums for x in pair]
    row = jnp.arange(local * block)
    sender, inner = row // (local * slots), row % (local * slots)
    source = (inner // slots) * block + sender * slots + inner % slots
    order = (source[:, None] == row[None, :]).astype(BF)
    flops = 2 * local * rows * units * width * len(weights)
    return pl.pallas_call(
        kernel,
        grid=(rows // step,),
        in_specs=[pl.BlockSpec((step, units), lambda i: (i, 0))] * len(inputs)
        + [pl.BlockSpec(w.shape, lambda i: (0, 0, 0)) for w in weights]
        + [pl.BlockSpec(order.shape, lambda i: (0, 0))],
        out_specs=pl.BlockSpec((local * step, width), lambda i: (i, 0)),
        out_shape=jax.ShapeDtypeStruct((local * rows, width), BF),
        compiler_params=pltpu.CompilerParams(vmem_limit_bytes=50 * 1024 * 1024),
        cost_estimate=pl.CostEstimate(flops=flops, bytes_accessed=12 * 1024 * 1024, transcendentals=local * rows * units),
    )(*inputs, *weights, order)


def shards(tokens, cotangent, routes, route_weights, gate_weight, up_weight, down_weight):
    ep = lax.axis_size("ep")
    ring = lax.axis_size("cp") * lax.axis_size("tp")
    local, width, units = gate_weight.shape
    own_tok, top = routes.shape
    group = own_tok * ring
    experts = local * ep
    slots = min(group, 5 * group * top // (4 * experts))
    rows = ep * slots

    high = lax.reduce_precision(route_weights, 8, 7)
    low = route_weights - high
    meta = jnp.concatenate([routes.astype(BF), high.astype(BF), low.astype(BF)], axis=1)
    meta = jnp.pad(meta, ((0, 0), (0, 128 - 3 * top)))
    tok_out = jnp.concatenate(
        [
            tokens.reshape(own_tok, ring, width).transpose(1, 0, 2),
            cotangent.reshape(own_tok, ring, width).transpose(1, 0, 2),
            jnp.broadcast_to(meta[None], (ring, own_tok, 128)),
        ],
        axis=2,
    )
    tok_in = lax.all_to_all(tok_out, Z, split_axis=0, concat_axis=0, tiled=True).reshape(group, 2 * width + 128)
    tok_cols = tok_in[:, :width]
    grad_cols = tok_in[:, width : 2 * width]
    meta = tok_in[:, 2 * width :]
    group_routes = meta[:, :top].astype(jnp.int32)
    group_weights = meta[:, top : 2 * top].astype(F32) + meta[:, 2 * top : 3 * top].astype(F32)

    named = group_routes[:, :, None] == jnp.arange(experts, dtype=jnp.int32)
    mask = jnp.any(named, axis=1)
    before = jnp.arange(group)[None, :] < jnp.arange(group)[:, None]
    position = dot(mask.astype(BF), before.astype(BF), ((0,), (1,))).astype(jnp.int32)
    position = jnp.where(mask.T, position, -1).reshape(ep, local, 1, group)
    slot = jnp.arange(slots, dtype=jnp.int32)
    hit = position == slot[:, None]
    spread = hit.astype(BF)
    def over_ep(out):
        return lax.all_to_all(out, "ep", split_axis=0, concat_axis=0, tiled=True)

    tok_rows, parts = [], []
    for e in range(local):
        out = dot(spread[:, e].reshape(rows, group), tok_cols, ((1,), (0,))).astype(BF)
        if e:
            out = after(out, *parts[0])
        tok_rows.append(over_ep(out.reshape(ep, slots, width)).reshape(rows, width))
        parts.append([dot(tok_rows[e], w[e], ((1,), (0,))).astype(BF) for w in (gate_weight, up_weight)])
    grad_cols = after(grad_cols, *parts[-1])
    out = dot(spread.reshape(local * rows, group), grad_cols, ((1,), (0,)))
    grad_send = out.astype(BF).reshape(ep, local * slots, width)
    grad_rows = over_ep(grad_send).reshape(ep, local, slots, width)

    first = [lax.psum(part, Z) for part in parts[0]]
    ways = (1, -1)
    back_parts = [
        dot(grad_rows[:, e].reshape(rows, width), down_weight[e], ((1,), (1,))).astype(BF) for e in range(local)
    ]
    second = ring_sum(
        [part.reshape(ring, rows // ring, units) for part in parts[1]], ways, {6: back_parts}
    )
    second = [after(chunk, *first) for chunk in second]
    backs = [lax.psum(part, Z[::-1]) for part in back_parts]
    second = [whole.reshape(rows, units) for whole in ring_spread(second, ways, ring)]
    gates, uppers = zip(first, second)

    def give_back(out):
        return over_ep(out.reshape(ep, local * slots, width)).reshape(local * rows, width)

    def combine(out):
        both = dot(gather, out, ((0,), (0,)))
        return (both[:group] + both[group:]).astype(BF)

    out_back = give_back(
        expert_rows(output_kernel, [gates, uppers], [down_weight], slots)
    )
    grads = expert_rows(grad_kernel, [gates, uppers, backs], [gate_weight, up_weight], slots)
    group_weights = after(group_weights, grads)
    weight = jnp.sum(jnp.where(named, group_weights[:, :, None], 0.0), axis=1)
    scaled = jnp.where(hit, weight.T.reshape(ep, local, 1, group), 0.0).reshape(local * rows, group)
    top_term = lax.reduce_precision(scaled, 8, 7)
    gather = jnp.concatenate([top_term.astype(BF), (scaled - top_term).astype(BF)], axis=1)
    grad_back = give_back(after(grads, out_back))
    cols = jnp.stack([combine(out_back), combine(grad_back)], axis=1).reshape(ring, own_tok, 2, width)
    mine = lax.all_to_all(cols, Z, split_axis=0, concat_axis=0, tiled=True)
    return (
        mine[:, :, 0].transpose(1, 0, 2).reshape(own_tok, ring * width),
        mine[:, :, 1].transpose(1, 0, 2).reshape(own_tok, ring * width),
    )


def solution(mesh):
    in_specs = (
        P(ALL, None),
        P(ALL, None),
        P(ALL, None),
        P(ALL, None),
        P("ep", Z, None),
        P("ep", Z, None),
        P("ep", None, Z),
    )
    out_specs = (P(ALL, None), P(ALL, None))
    return jax.shard_map(shards, mesh=mesh, in_specs=in_specs, out_specs=out_specs, check_vma=False)
```

```python
import jax
import jax.numpy as jnp
from jax import lax
from jax.experimental import pallas as pl
from jax.experimental.pallas import tpu as pltpu
from jax.sharding import PartitionSpec as P

BF = jnp.bfloat16
F32 = jnp.float32
Z = ("cp", "tp")
ALL = ("ep", "cp", "tp")


def ring_pairs(step):
    cp, tp = lax.axis_size("cp"), lax.axis_size("tp")
    count = cp * tp

    def place(z):
        z = z % count
        return (z % cp) * tp + z // cp

    return [(place(z), place(z + step)) for z in range(count)]


def ring_place():
    return lax.axis_index("tp") * lax.axis_size("cp") + lax.axis_index("cp")


def chunk_of(part, index):
    count = part.shape[0]
    return lax.dynamic_index_in_dim(part, lax.rem(index + 2 * count, count), 0, keepdims=False)


def ring_sum(parts, steps, ties):
    count = parts[0].shape[0]
    place, pairs = ring_place(), [ring_pairs(step) for step in steps]
    totals = [chunk_of(part, place - step) for part, step in zip(parts, steps)]
    for hop in range(count - 1):
        totals = [after(total, *ties.get(hop, ())) for total in totals]
        got = [lax.ppermute(total, Z, pair) for total, pair in zip(totals, pairs)]
        own = [chunk_of(part, place - step * (2 + hop)) for part, step in zip(parts, steps)]
        totals = [(g.astype(F32) + o.astype(F32)).astype(BF) for g, o in zip(got, own)]
    return totals


def ring_spread(chunks, steps, count):
    place, pairs = ring_place(), [ring_pairs(step) for step in steps]
    wholes = [jnp.zeros((count,) + chunk.shape, chunk.dtype) for chunk in chunks]
    for hop in range(count):
        if hop:
            chunks = [lax.ppermute(chunk, Z, pair) for chunk, pair in zip(chunks, pairs)]
        at = [lax.rem(place - step * hop + 2 * count, count) for step in steps]
        wholes = [lax.dynamic_update_index_in_dim(w, c, i, 0) for w, c, i in zip(wholes, chunks, at)]
    return wholes


def after(x, *others):
    if not others:
        return x
    return lax.optimization_barrier((x,) + others)[0]


def dot(a, b, dims):
    return lax.dot_general(a, b, (dims, ((), ())), preferred_element_type=F32)


def interleave(rows, order, out):
    step = order.shape[0]
    piece = step // len(rows)
    for i in range(out.shape[0] // step):
        both = jnp.concatenate([r[i * piece : (i + 1) * piece] for r in rows], axis=0)
        out[i * step : (i + 1) * step, :] = dot(order[...], both, ((1,), (0,))).astype(BF)


def output_kernel(*refs):
    (gate0, gate1, up0, up1, down, order, out) = refs
    rows = []
    for e, (gate, upper) in enumerate(((gate0, up0), (gate1, up1))):
        gate, upper = gate[...].astype(F32), upper[...].astype(F32)
        hidden = (gate * jax.nn.sigmoid(gate) * upper).astype(BF)
        rows.append(dot(hidden, down[e], ((1,), (0,))).astype(BF))
    interleave(rows, order, out)


def grad_kernel(*refs):
    (gate0, gate1, up0, up1, back0, back1, gate_w, up_w, order, out) = refs
    rows = []
    for e, (gate, upper, back) in enumerate(((gate0, up0, back0), (gate1, up1, back1))):
        gate, upper, back = (x[...].astype(F32) for x in (gate, upper, back))
        sig = jax.nn.sigmoid(gate)
        d_up = (back * gate * sig).astype(BF)
        d_gate = (back * upper * sig * (1.0 + gate * (1.0 - sig))).astype(BF)
        grad = dot(d_gate, gate_w[e], ((1,), (1,))) + dot(d_up, up_w[e], ((1,), (1,)))
        rows.append(grad.astype(BF))
    interleave(rows, order, out)


def expert_rows(kernel, sums, weights, slots):
    rows, units = sums[0][0].shape
    local = weights[0].shape[0]
    width = weights[0].size // (local * units)
    block = 8 * slots
    step = 2 * block
    inputs = [x for pair in sums for x in pair]
    row = jnp.arange(local * block)
    sender, inner = row // (local * slots), row % (local * slots)
    source = (inner // slots) * block + sender * slots + inner % slots
    order = (source[:, None] == row[None, :]).astype(BF)
    flops = 2 * local * rows * units * width * len(weights)
    return pl.pallas_call(
        kernel,
        grid=(rows // step,),
        in_specs=[pl.BlockSpec((step, units), lambda i: (i, 0))] * len(inputs)
        + [pl.BlockSpec(w.shape, lambda i: (0, 0, 0)) for w in weights]
        + [pl.BlockSpec(order.shape, lambda i: (0, 0))],
        out_specs=pl.BlockSpec((local * step, width), lambda i: (i, 0)),
        out_shape=jax.ShapeDtypeStruct((local * rows, width), BF),
        compiler_params=pltpu.CompilerParams(vmem_limit_bytes=50 * 1024 * 1024),
        cost_estimate=pl.CostEstimate(flops=flops, bytes_accessed=12 * 1024 * 1024, transcendentals=local * rows * units),
    )(*inputs, *weights, order)


def shards(tokens, cotangent, routes, route_weights, gate_weight, up_weight, down_weight):
    ep = lax.axis_size("ep")
    ring = lax.axis_size("cp") * lax.axis_size("tp")
    local, width, units = gate_weight.shape
    own_tok, top = routes.shape
    group = own_tok * ring
    experts = local * ep
    slots = min(group, 5 * group * top // (4 * experts))
    rows = ep * slots

    high = lax.reduce_precision(route_weights, 8, 7)
    low = route_weights - high
    meta = jnp.concatenate([routes.astype(BF), high.astype(BF), low.astype(BF)], axis=1)
    meta = jnp.pad(meta, ((0, 0), (0, 128 - 3 * top)))
    tok_out = jnp.concatenate(
        [
            tokens.reshape(own_tok, ring, width).transpose(1, 0, 2),
            cotangent.reshape(own_tok, ring, width).transpose(1, 0, 2),
            jnp.broadcast_to(meta[None], (ring, own_tok, 128)),
        ],
        axis=2,
    )
    tok_in = lax.all_to_all(tok_out, Z, split_axis=0, concat_axis=0, tiled=True).reshape(group, 2 * width + 128)
    tok_cols = tok_in[:, :width]
    grad_cols = tok_in[:, width : 2 * width]
    meta = tok_in[:, 2 * width :]
    group_routes = meta[:, :top].astype(jnp.int32)
    group_weights = meta[:, top : 2 * top].astype(F32) + meta[:, 2 * top : 3 * top].astype(F32)

    named = group_routes[:, :, None] == jnp.arange(experts, dtype=jnp.int32)
    mask = jnp.any(named, axis=1)
    before = jnp.arange(group)[None, :] < jnp.arange(group)[:, None]
    position = dot(mask.astype(BF), before.astype(BF), ((0,), (1,))).astype(jnp.int32)
    position = jnp.where(mask.T, position, -1).reshape(ep, local, 1, group)
    slot = jnp.arange(slots, dtype=jnp.int32)
    hit = position == slot[:, None]
    spread = hit.astype(BF)
    def over_ep(out):
        return lax.all_to_all(out, "ep", split_axis=0, concat_axis=0, tiled=True)

    tok_rows, parts = [], []
    for e in range(local):
        out = dot(spread[:, e].reshape(rows, group), tok_cols, ((1,), (0,))).astype(BF)
        if e:
            out = after(out, *parts[0])
        tok_rows.append(over_ep(out.reshape(ep, slots, width)).reshape(rows, width))
        parts.append([dot(tok_rows[e], w[e], ((1,), (0,))).astype(BF) for w in (gate_weight, up_weight)])
    grad_cols = after(grad_cols, tok_rows[-1])
    out = dot(spread.reshape(local * rows, group), grad_cols, ((1,), (0,)))
    grad_send = out.astype(BF).reshape(ep, local * slots, width)
    grad_rows = over_ep(grad_send).reshape(ep, local, slots, width)

    first = [lax.psum(part, Z) for part in parts[0]]
    ways = (1, -1)
    back_parts = [
        dot(grad_rows[:, e].reshape(rows, width), down_weight[e], ((1,), (1,))).astype(BF) for e in range(local)
    ]
    second = ring_sum(
        [part.reshape(ring, rows // ring, units) for part in parts[1]], ways, {5: back_parts}
    )
    second = [after(chunk, *first) for chunk in second]
    backs = [lax.psum(part, Z[::-1]) for part in back_parts]
    second = [whole.reshape(rows, units) for whole in ring_spread(second, ways, ring)]
    gates, uppers = zip(first, second)

    def give_back(out):
        return over_ep(out.reshape(ep, local * slots, width)).reshape(local * rows, width)

    def combine(out):
        both = dot(gather, out, ((0,), (0,)))
        return (both[:group] + both[group:]).astype(BF)

    out_back = give_back(
        expert_rows(output_kernel, [gates, uppers], [down_weight], slots)
    )
    grads = expert_rows(grad_kernel, [gates, uppers, backs], [gate_weight, up_weight], slots)
    group_weights = after(group_weights, grads)
    weight = jnp.sum(jnp.where(named, group_weights[:, :, None], 0.0), axis=1)
    scaled = jnp.where(hit, weight.T.reshape(ep, local, 1, group), 0.0).reshape(local * rows, group)
    top_term = lax.reduce_precision(scaled, 8, 7)
    gather = jnp.concatenate([top_term.astype(BF), (scaled - top_term).astype(BF)], axis=1)
    grad_back = give_back(after(grads, out_back))
    cols = jnp.stack([combine(out_back), combine(grad_back)], axis=1).reshape(ring, own_tok, 2, width)
    mine = lax.all_to_all(cols, Z, split_axis=0, concat_axis=0, tiled=True)
    return (
        mine[:, :, 0].transpose(1, 0, 2).reshape(own_tok, ring * width),
        mine[:, :, 1].transpose(1, 0, 2).reshape(own_tok, ring * width),
    )


def solution(mesh):
    in_specs = (
        P(ALL, None),
        P(ALL, None),
        P(ALL, None),
        P(ALL, None),
        P("ep", Z, None),
        P("ep", Z, None),
        P("ep", None, Z),
    )
    out_specs = (P(ALL, None), P(ALL, None))
    return jax.shard_map(shards, mesh=mesh, in_specs=in_specs, out_specs=out_specs, check_vma=False)
```
